32 devices in a mesh: grp: 2 (over y), sec: 4 (over z), term: 4 (over x, core).
Axes of the slice: x: 2, y: 2, z: 4, core: 2. Of those that a mesh axis runs over, the one named last changes fastest.
Arguments:
- trial_vectors: bfloat16 [2, 8, 4, 128, 128], P(None, ('grp', 'sec')), parts along dimension 1, may hold values from -30 to 30
- left_ops: bfloat16 [8, 8, 128, 128], P('term', ('grp', 'sec')), parts along dimension 1, may hold values from -2 to 2, as said below
- right_ops: bfloat16 [8, 8, 128, 128], P('term', ('grp', 'sec')), parts along dimension 1, may hold values from -2 to 2, as said below
- term_mask: int32 [8, 8], P('term', ('grp', 'sec')), parts along dimension 1, may hold values 0 or 1
Outputs:
- residual: bfloat16 [2, 8, 4, 128, 128], P(None, ('grp', 'sec'), 'term'), parts along dimension 1
- subspace: float32 [4, 2], P('grp'), parts along dimension 0
The draws below stay inside these ranges and needn't reach their ends.
There are 2 independent parts, one for each index of `grp`. The reference program is written for one: setup_inputs(seed, part) draws one part's arguments, and reference() takes and returns one part's arrays. A program takes and returns all parts, laid end to end along the dimension named above; each array names one. Nothing has to cross between parts.
Inputs may be any that keep to these rules, and one draw needn't show every extreme that they name: `left_ops`: environment operator blocks. `right_ops`: environment operator blocks.
All inputs are finite; a program needn't handle non-finite values. No bound on the sum of `term_mask` on one device may be relied on, other than what follows from the above.
Results may differ from the reference program's by a relative error of at most 0.0052.
Values may be sent and summed in bfloat16 or wider, within the bound.
A program may use at most 64 MiB of HBM per device.

```python
import math
import jax
import jax.numpy as jnp
from jax import lax

B = 128
NV = 2
K = 8
NS = 4


def index_ramp():
    return jnp.arange(B, dtype=jnp.float32) * (2.0 / (B - 1)) - 1.0


def block_ops(key, count, sectors, diag_lo, diag_hi):
    noise_part = jnp.clip(jax.random.normal(key, (count, sectors, B, B), jnp.float32), -4.0, 4.0) * (0.5 / math.sqrt(B))
    diagonal = jax.random.uniform(jax.random.fold_in(key, 7), (count, sectors), jnp.float32, diag_lo, diag_hi)
    profile = 0.2 + 0.9 * (index_ramp() + 1.0)
    shaped = jnp.eye(B, dtype=jnp.float32) * profile[None, :]
    total = (noise_part + diagonal[:, :, None, None] * shaped) / math.sqrt(count)
    return jnp.clip(total, -2.0, 2.0).astype(jnp.bfloat16)


def draw_left_ops(key, part):
    key = jax.random.fold_in(key, 1)
    return block_ops(key, K, NS, 0.5, 1.5)


def draw_right_ops(key, part):
    key = jax.random.fold_in(key, 2)
    return block_ops(key, K, NS, 0.5, 1.5)


def shape_vectors(others):
    coupled = 0.6 * others[0:1] + 0.8 * others
    mixed = jnp.concatenate([others[0:1], coupled[1:]], axis=0)
    weight = jnp.exp(index_ramp())
    return (mixed * weight[:, None] * weight[None, :]).astype(jnp.bfloat16)


def draw_trial_vectors(key, part):
    key = jax.random.fold_in(key, 3)
    others = jnp.clip(jax.random.normal(key, (NV, NS, NS, B, B), jnp.float32), -3.5, 3.5)
    return shape_vectors(others)


def set_ends(array, stream_key, least, largest):
    extent = array.shape
    spot = [jax.random.randint(jax.random.fold_in(stream_key, axis), (), 0, extent[axis]) for axis in range(len(extent))]
    array = array.at[tuple(spot)].set(least)
    longest = extent.index(max(extent))
    spot[longest] = (spot[longest] + 1) % extent[longest]
    return array.at[tuple(spot)].set(largest)


def setup_inputs(seed: int = 0, part: int = 0) -> dict:
    keys = jax.random.split(jax.random.key(seed), 5)
    part_keys = jax.random.split(jax.random.fold_in(keys[4], part), 5)
    return {
        "trial_vectors": draw_trial_vectors(jax.random.fold_in(jax.random.fold_in(keys[4], part), 71), part),
        "left_ops": draw_left_ops(jax.random.fold_in(jax.random.fold_in(keys[4], part), 71), part),
        "right_ops": draw_right_ops(jax.random.fold_in(jax.random.fold_in(keys[4], part), 71), part),
        "term_mask": set_ends((jax.random.randint(part_keys[3], (K, NS), 0, 4) < 3).astype(jnp.int32), jax.random.fold_in(part_keys[3], 1), 0, 1),
    }


def reference(trial_vectors, left_ops, right_ops, term_mask):
    left_mat = left_ops * term_mask[:, :, None, None].astype(jnp.bfloat16)
    vec_wide = trial_vectors.astype(jnp.float32)

    def advance(running, pieces):
        left_op, right_op = pieces
        left_blocks = jnp.einsum("aij,vabjc->vabic", left_op.astype(jnp.float32), vec_wide).astype(jnp.bfloat16)
        added = jnp.einsum("vabic,bdc->vabid", left_blocks.astype(jnp.float32), right_op.astype(jnp.float32))
        return running + added, None

    sigma_full, _ = lax.scan(advance, jnp.zeros(trial_vectors.shape, jnp.float32), (left_mat, right_ops))
    cell_count = jnp.float32(NS * NS * B * B)
    subspace = jnp.einsum("vabic,wabic->vw", vec_wide, sigma_full, precision=lax.Precision.HIGHEST) / cell_count
    norms = jnp.sum(vec_wide * vec_wide, axis=(1, 2, 3, 4)) / cell_count
    ritz_values = jnp.diagonal(subspace) / norms
    residual = (sigma_full - ritz_values[:, None, None, None, None] * vec_wide).astype(jnp.bfloat16)
    return residual, subspace
```

```python
import functools

import jax
import jax.numpy as jnp
from jax import lax
from jax.experimental import pallas as pl
from jax.experimental.pallas import tpu as pltpu
from jax.sharding import PartitionSpec as P

MESH = pl.DeviceIdType.MESH
F32 = jnp.float32
BF16 = jnp.bfloat16


def each(count, body, first=0):
    if count - first <= 16:
        for index in range(first, count):
            body(index)
    else:
        lax.fori_loop(first, count, lambda index, carry: (body(index), carry)[1], 0)


def kernel(
    sectors, terms, x_hbm, l_hbm, r_hbm, mask_ref, out_ref, sub_ref,
    x_buf, l_buf, r_own, r_buf, t_buf, stat, stat_buf,
    in_sem, l_send, l_recv, r_send, r_recv, s_send, s_recv,
):
    vectors, share, size = x_buf.shape[0], x_buf.shape[1], x_buf.shape[2]
    ops = r_own.shape[0]
    sec, term = lax.axis_index("sec"), lax.axis_index("term")
    group = sectors * terms

    def peer(step):
        there = lax.rem(sec * terms + term + step, group)
        return {"sec": there // terms, "term": lax.rem(there, terms)}

    l_in = pltpu.make_async_copy(l_hbm.at[:, 0], l_buf.at[0], in_sem.at[0])
    r_in = pltpu.make_async_copy(r_hbm.at[:, 0], r_own, in_sem.at[1])
    x_in = pltpu.make_async_copy(
        x_hbm.at[:, 0, pl.ds(term * share, share)], x_buf, in_sem.at[2]
    )
    r_in.start()
    l_in.start()
    x_in.start()

    barrier = pltpu.get_barrier_semaphore()

    def greet(step):
        pl.semaphore_signal(barrier, inc=1, device_id=peer(step), device_id_type=MESH)

    each(group, greet, 1)

    l_in.wait()
    for k in range(ops):
        keep = mask_ref[k, 0].astype(F32)
        l_buf[0, k] = (l_buf[0, k].astype(F32) * keep).astype(BF16)
    r_in.wait()
    pl.semaphore_wait(barrier, group - 1)

    owner = sec // share
    r_slot = lax.rem(owner - term + terms, terms) * share + lax.rem(sec, share)

    def r_copy(step, slot):
        return pltpu.make_async_remote_copy(
            src_ref=r_own,
            dst_ref=r_buf.at[slot],
            send_sem=r_send.at[step],
            recv_sem=r_recv.at[slot],
            device_id={"sec": lax.rem(sec + step, sectors), "term": owner},
            device_id_type=MESH,
        )

    def l_copy(step):
        return pltpu.make_async_remote_copy(
            src_ref=l_buf.at[0],
            dst_ref=l_buf.at[step],
            send_sem=l_send.at[step],
            recv_sem=l_recv.at[step],
            device_id={"sec": sec, "term": lax.rem(term + step, terms)},
            device_id_type=MESH,
        )

    each(sectors, lambda step: r_copy(step, r_slot).start(), 1)
    each(terms, lambda step: l_copy(step).start(), 1)

    @pl.when(owner != term)
    def _():
        r_copy(0, r_slot).start()

    @pl.when(owner == term)
    def _():
        pltpu.make_async_copy(r_own, r_buf.at[r_slot], r_recv.at[r_slot]).start()

    x_in.wait()
    x_wide = jnp.concatenate(
        [x_buf[v, b] for b in range(share) for v in range(vectors)], axis=1
    )

    def left(step):
        part = jnp.dot(
            l_buf[step].reshape(ops * size, size), x_wide, preferred_element_type=F32
        ).astype(BF16)
        for b in range(share):
            for v in range(vectors):
                at = (b * vectors + v) * size
                for k in range(ops):
                    t_buf[step, b, v * size:(v + 1) * size, k * size:(k + 1) * size] = part[
                        k * size:(k + 1) * size, at:at + size
                    ]

    left(0)
    for step in range(1, terms):
        l_copy(step).wait_recv()
        left(step)

    stat_rows = [jnp.zeros((1, size), F32)] * 8
    sigmas = []
    for b in range(share):
        sigma = jnp.zeros((vectors * size, size), F32)
        for step in range(terms):
            slot = step * share + b
            r_copy(0, slot).wait_recv()
            right = jnp.concatenate([r_buf[slot, k] for k in range(ops)], axis=1)
            sigma += lax.dot_general(
                t_buf[step, b], right, (((1,), (1,)), ((), ())), preferred_element_type=F32
            )
        sigmas.append(sigma)
        xs = [x_buf[v, b].astype(F32) for v in range(vectors)]
        for v in range(vectors):
            for w in range(vectors):
                stat_rows[v * vectors + w] += jnp.sum(
                    xs[v] * sigma[w * size:(w + 1) * size], axis=0, keepdims=True
                )
            stat_rows[vectors * vectors + v] += jnp.sum(xs[v] * xs[v], axis=0, keepdims=True)
    stat[...] = jnp.concatenate(stat_rows, axis=0)

    me = sec * terms + term

    def s_copy(step):
        return pltpu.make_async_remote_copy(
            src_ref=stat,
            dst_ref=stat_buf.at[me],
            send_sem=s_send.at[step],
            recv_sem=s_recv.at[me],
            device_id=peer(step),
            device_id_type=MESH,
        )

    each(group, lambda step: s_copy(step).start(), 1)
    pltpu.make_async_copy(stat, stat_buf.at[me], s_recv.at[me]).start()

    def s_wait(slot):
        pltpu.make_async_copy(stat, stat_buf.at[slot], s_recv.at[slot]).wait()

    each(group, s_wait)
    total = jnp.sum(jnp.sum(stat_buf[...], axis=0), axis=1, keepdims=True)
    total = total / F32(sectors * sectors * size * size)
    for v in range(vectors):
        for w in range(vectors):
            sub_ref[v:v + 1, w:w + 1] = total[v * vectors + w:v * vectors + w + 1]
    for v in range(vectors):
        own = v * vectors + v
        norm = vectors * vectors + v
        ritz = total[own:own + 1] / total[norm:norm + 1]
        for b in range(share):
            out_ref[v, 0, b] = (
                sigmas[b][v * size:(v + 1) * size] - ritz * x_buf[v, b].astype(F32)
            ).astype(BF16)

    each(sectors, lambda step: r_copy(step, r_slot).wait_send(), 1)
    each(terms, lambda step: l_copy(step).wait_send(), 1)
    each(group, lambda step: s_copy(step).wait_send(), 1)

    @pl.when(owner != term)
    def _():
        r_copy(0, r_slot).wait_send()


def local(sectors, terms, trial_vectors, left_ops, right_ops, term_mask):
    vectors, _, columns, size, _ = trial_vectors.shape
    ops = left_ops.shape[0]
    share = columns // terms
    group = sectors * terms
    any_space = pl.BlockSpec(memory_space=pl.ANY)
    return pl.pallas_call(
        functools.partial(kernel, sectors, terms),
        out_shape=(
            jax.ShapeDtypeStruct((vectors, 1, share, size, size), BF16),
            jax.ShapeDtypeStruct((vectors, vectors), F32),
        ),
        in_specs=[any_space, any_space, any_space, pl.BlockSpec(memory_space=pltpu.SMEM)],
        out_specs=(
            pl.BlockSpec(memory_space=pltpu.VMEM),
            pl.BlockSpec(memory_space=pltpu.VMEM),
        ),
        scratch_shapes=[
            pltpu.VMEM((vectors, share, size, size), BF16),
            pltpu.VMEM((terms, ops, size, size), BF16),
            pltpu.VMEM((ops, size, size), BF16),
            pltpu.VMEM((terms * share, ops, size, size), BF16),
            pltpu.VMEM((terms, share, vectors * size, ops * size), BF16),
            pltpu.VMEM((8, size), F32),
            pltpu.VMEM((group, 8, size), F32),
            pltpu.SemaphoreType.DMA((3,)),
            pltpu.SemaphoreType.DMA((terms,)),
            pltpu.SemaphoreType.DMA((terms,)),
            pltpu.SemaphoreType.DMA((sectors,)),
            pltpu.SemaphoreType.DMA((terms * share,)),
            pltpu.SemaphoreType.DMA((group,)),
            pltpu.SemaphoreType.DMA((group,)),
        ],
        compiler_params=pltpu.CompilerParams(
            collective_id=0, has_side_effects=True, vmem_limit_bytes=32 * 1024 * 1024
        ),
    )(trial_vectors, left_ops, right_ops, term_mask)


def solution(mesh):
    placed = (
        P(None, ("grp", "sec"), None, None, None),
        P("term", ("grp", "sec"), None, None),
        P("term", ("grp", "sec"), None, None),
        P("term", ("grp", "sec")),
    )
    return jax.shard_map(
        functools.partial(local, mesh.shape["sec"], mesh.shape["term"]),
        mesh=mesh,
        in_specs=placed,
        out_specs=(P(None, ("grp", "sec"), "term", None, None), P("grp", None)),
        check_vma=False,
    )
```

```python
import functools

import jax
import jax.numpy as jnp
from jax import lax
from jax.experimental import pallas as pl
from jax.experimental.pallas import tpu as pltpu
from jax.sharding import PartitionSpec as P

MESH = pl.DeviceIdType.MESH
F32 = jnp.float32
BF16 = jnp.bfloat16


def each(count, body, first=0):
    if count - first <= 16:
        for index in range(first, count):
            body(index)
    else:
        lax.fori_loop(first, count, lambda index, carry: (body(index), carry)[1], 0)


def kernel(
    sectors, terms, x_hbm, l_hbm, r_hbm, mask_hbm, out_ref, sub_ref,
    mask_ref, x_buf, l_buf, r_buf, r_more, t_buf, stat_buf,
    in_sem, l_send, l_recv, up_send, down_send, r_recv, more_send, more_recv, s_send, s_recv,
):
    vectors, share, size = x_buf.shape[0], x_buf.shape[1], x_buf.shape[2]
    ops = r_buf.shape[1]
    sec, term = lax.axis_index("sec"), lax.axis_index("term")
    pair, side = lax.div(term, 2), lax.rem(term, 2)
    pairs = terms // 2
    group = sectors * terms
    me = sec * terms + term

    def peer(step):
        there = lax.rem(me + step, group)
        return {"sec": lax.div(there, terms), "term": lax.rem(there, terms)}

    mask_in = pltpu.make_async_copy(mask_hbm, mask_ref, in_sem.at[3])
    l_in = pltpu.make_async_copy(l_hbm.at[:, 0], l_buf.at[term], in_sem.at[0])
    r_in = pltpu.make_async_copy(r_hbm.at[:, 0], r_buf.at[sec], in_sem.at[1])
    x_in = pltpu.make_async_copy(
        x_hbm.at[:, 0, pl.ds(term * share, share)], x_buf, in_sem.at[2]
    )
    mask_in.start()
    l_in.start()
    r_in.start()
    x_in.start()

    barrier = pltpu.get_barrier_semaphore()

    def greet(step):
        pl.semaphore_signal(barrier, inc=1, device_id=peer(step), device_id_type=MESH)

    each(group, greet, 1)

    mask_in.wait()
    l_in.wait()
    for k in range(ops):
        keep = mask_ref[0, k].astype(F32)
        l_buf[term, k] = (l_buf[term, k].astype(F32) * keep).astype(BF16)
    r_in.wait()
    pl.semaphore_wait(barrier, group - 1)

    def up_copy(block):
        return pltpu.make_async_remote_copy(
            src_ref=r_buf.at[block],
            dst_ref=r_buf.at[block],
            send_sem=up_send.at[block],
            recv_sem=r_recv.at[block],
            device_id={"sec": sec + 1, "term": term},
            device_id_type=MESH,
        )

    def down_copy(block):
        return pltpu.make_async_remote_copy(
            src_ref=r_buf.at[block],
            dst_ref=r_buf.at[block],
            send_sem=down_send.at[block],
            recv_sem=r_recv.at[block],
            device_id={"sec": sec - 1, "term": term},
            device_id_type=MESH,
        )

    def more_copy(block):
        owner = lax.div(block, share)
        far = lax.rem(lax.div(owner, 2) - pair + pairs, pairs)
        other = lax.rem(lax.rem(owner, 2) + side, 2)
        slot = (2 * far + other - 1) * share + lax.rem(block, share)
        return pltpu.make_async_remote_copy(
            src_ref=r_buf.at[block],
            dst_ref=r_more.at[slot],
            send_sem=more_send.at[block],
            recv_sem=more_recv.at[slot],
            device_id={"sec": sec, "term": owner},
            device_id_type=MESH,
        )

    def source(relation):
        far, other = relation // 2, relation % 2
        there = lax.rem(pair - far + pairs, pairs)
        return 2 * there + (1 - side if other else side)

    def l_copy(block, far, other):
        return pltpu.make_async_remote_copy(
            src_ref=l_buf.at[block],
            dst_ref=l_buf.at[block],
            send_sem=l_send.at[2 * block + other],
            recv_sem=l_recv.at[block],
            device_id={
                "sec": sec,
                "term": 2 * lax.rem(pair + far, pairs) + (1 - side if other else side),
            },
            device_id_type=MESH,
        )

    def l_far(far):
        return pltpu.make_async_remote_copy(
            src_ref=l_buf.at[term],
            dst_ref=l_buf.at[term],
            send_sem=l_send.at[2 * terms + far],
            recv_sem=l_recv.at[term],
            device_id={"sec": sec, "term": 2 * lax.rem(pair + far, pairs) + side},
            device_id_type=MESH,
        )

    def walk(step, act):
        if step == 0:
            steps = ((sec, True, True),)
        else:
            steps = ((sec - step, True, False), (sec + step, False, True))
        for block, up, down in steps:
            @pl.when((block >= 0) & (block < sectors))
            def _():
                if step and act == "go":
                    up_copy(block).wait_recv()
                for on, edge, copy in (
                    (up, sec + 1 < sectors, up_copy),
                    (down, sec >= 1, down_copy),
                    (True, lax.div(block, share) != term, more_copy),
                ):
                    if on:
                        @pl.when(edge)
                        def _():
                            if act == "go":
                                copy(block).start()
                            else:
                                copy(block).wait_send()

    walk(0, "go")
    for far in range(1, pairs):
        l_far(far).start()
    l_copy(term, 0, 1).start()

    x_in.wait()
    x_wide = jnp.concatenate(
        [x_buf[v, b] for b in range(share) for v in range(vectors)], axis=1
    )

    def left(relation):
        part = jnp.dot(
            l_buf[source(relation)].reshape(ops * size, size), x_wide,
            preferred_element_type=F32,
        ).astype(BF16)
        for b in range(share):
            for v in range(vectors):
                at = (b * vectors + v) * size
                for k in range(ops):
                    t_buf[relation, b, v * size:(v + 1) * size, k * size:(k + 1) * size] = part[
                        k * size:(k + 1) * size, at:at + size
                    ]

    left(0)
    if sectors > 1:
        walk(1, "go")
    for far in range(1, pairs):
        block = source(2 * far)
        l_copy(block, 0, 1).wait_recv()
        l_copy(block, 0, 1).start()
    for step in range(2, sectors):
        walk(step, "go")
        if step == 2:
            for far in range(1, pairs):
                left(2 * far)
    l_copy(source(1), 0, 1).wait_recv()
    left(1)
    for far in range(1, pairs):
        l_copy(source(2 * far + 1), 0, 1).wait_recv()
        left(2 * far + 1)
        if sectors <= 2:
            left(2 * far)

    stat_rows = [jnp.zeros((1, size), F32)] * 8
    sigmas = []
    for b in range(share):
        sigma = jnp.zeros((vectors * size, size), F32)
        for relation in range(terms):
            if relation:
                ref = r_more.at[(relation - 1) * share + b]
                pltpu.make_async_copy(ref, ref, more_recv.at[(relation - 1) * share + b]).wait()
            else:
                ref = r_buf.at[term * share + b]
            right = jnp.concatenate([ref[k] for k in range(ops)], axis=1)
            sigma += lax.dot_general(
                t_buf[relation, b], right, (((1,), (1,)), ((), ())),
                preferred_element_type=F32,
            )
        sigmas.append(sigma)
        xs = [x_buf[v, b].astype(F32) for v in range(vectors)]
        for v in range(vectors):
            for w in range(vectors):
                stat_rows[v * vectors + w] += jnp.sum(
                    xs[v] * sigma[w * size:(w + 1) * size], axis=0, keepdims=True
                )
            stat_rows[vectors * vectors + v] += jnp.sum(xs[v] * xs[v], axis=0, keepdims=True)
    sums = jnp.sum(jnp.concatenate(stat_rows, axis=0), axis=1, keepdims=True)
    here = lax.broadcasted_iota(jnp.int32, (8, size), 0)
    lane = lax.broadcasted_iota(jnp.int32, (8, size), 1)
    stat_buf[me] = jnp.sum(jnp.where(here == lane, sums, 0.0), axis=0, keepdims=True)

    def s_copy(step):
        return pltpu.make_async_remote_copy(
            src_ref=stat_buf.at[me],
            dst_ref=stat_buf.at[me],
            send_sem=s_send,
            recv_sem=s_recv,
            device_id=peer(step),
            device_id_type=MESH,
        )

    each(group, lambda step: s_copy(step).start(), 1)
    others = stat_buf.at[pl.ds(0, group - 1)]
    pltpu.make_async_copy(others, others, s_recv).wait()
    total = jnp.sum(stat_buf[...], axis=0) / F32(sectors * sectors * size * size)
    for v in range(vectors):
        sub_ref[v:v + 1, :] = total[:, v * vectors:(v + 1) * vectors]
    for v in range(vectors):
        own = v * vectors + v
        norm = vectors * vectors + v
        ritz = total[:, own:own + 1] / total[:, norm:norm + 1]
        for b in range(share):
            out_ref[v, 0, b] = (
                sigmas[b][v * size:(v + 1) * size] - ritz * x_buf[v, b].astype(F32)
            ).astype(BF16)

    for step in range(sectors):
        walk(step, "end")
    for far in range(1, pairs):
        l_far(far).wait_send()
    for far in range(pairs):
        l_copy(source(2 * far), 0, 1).wait_send()
    pltpu.make_async_copy(others, others, s_send).wait()


def local(sectors, terms, trial_vectors, left_ops, right_ops, term_mask):
    vectors, _, columns, size, _ = trial_vectors.shape
    ops = left_ops.shape[0]
    share = columns // terms
    group = sectors * terms
    hbm = pl.BlockSpec(memory_space=pltpu.HBM)
    return pl.pallas_call(
        functools.partial(kernel, sectors, terms),
        out_shape=(
            jax.ShapeDtypeStruct((vectors, 1, share, size, size), BF16),
            jax.ShapeDtypeStruct((vectors, vectors), F32),
        ),
        in_specs=[hbm] * 4,
        out_specs=(
            pl.BlockSpec(memory_space=pltpu.VMEM),
            pl.BlockSpec(memory_space=pltpu.VMEM),
        ),
        scratch_shapes=[
            pltpu.SMEM((1, ops), jnp.int32),
            pltpu.VMEM((vectors, share, size, size), BF16),
            pltpu.VMEM((terms, ops, size, size), BF16),
            pltpu.VMEM((columns, ops, size, size), BF16),
            pltpu.VMEM(((terms - 1) * share, ops, size, size), BF16),
            pltpu.VMEM((terms, share, vectors * size, ops * size), BF16),
            pltpu.VMEM((group, 1, size), F32),
            pltpu.SemaphoreType.DMA((4,)),
            pltpu.SemaphoreType.DMA((2 * terms + terms // 2,)),
            pltpu.SemaphoreType.DMA((terms,)),
            pltpu.SemaphoreType.DMA((columns,)),
            pltpu.SemaphoreType.DMA((columns,)),
            pltpu.SemaphoreType.DMA((columns,)),
            pltpu.SemaphoreType.DMA((columns,)),
            pltpu.SemaphoreType.DMA(((terms - 1) * share,)),
            pltpu.SemaphoreType.DMA,
            pltpu.SemaphoreType.DMA,
        ],
        compiler_params=pltpu.CompilerParams(
            collective_id=0, has_side_effects=True, vmem_limit_bytes=64 * 1024 * 1024
        ),
    )(trial_vectors, left_ops, right_ops, term_mask.T)


def solution(mesh):
    placed = (
        P(None, ("grp", "sec"), None, None, None),
        P("term", ("grp", "sec"), None, None),
        P("term", ("grp", "sec"), None, None),
        P("term", ("grp", "sec")),
    )
    return jax.shard_map(
        functools.partial(local, mesh.shape["sec"], mesh.shape["term"]),
        mesh=mesh,
        in_specs=placed,
        out_specs=(P(None, ("grp", "sec"), "term", None, None), P("grp", None)),
        check_vma=False,
    )
```

```python
import functools

import jax
import jax.numpy as jnp
from jax import lax
from jax.experimental import pallas as pl
from jax.experimental.pallas import tpu as pltpu
from jax.sharding import PartitionSpec as P

MESH = pl.DeviceIdType.MESH
F32 = jnp.float32
BF16 = jnp.bfloat16


def each(count, body, first=0):
    if count - first <= 16:
        for index in range(first, count):
            body(index)
    else:
        lax.fori_loop(first, count, lambda index, carry: (body(index), carry)[1], 0)


def kernel(
    sectors, terms, x_hbm, l_hbm, r_hbm, mask_hbm, out_hbm, sub_hbm,
    out_ref, sub_ref, mask_ref, x_buf, l_buf, r_own, r_buf, t_buf, stat_buf,
    in_sem, l_send, l_recv, r_send, r_recv, s_send, s_recv,
):
    vectors, share, size = x_buf.shape[0], x_buf.shape[1], x_buf.shape[2]
    ops = r_own.shape[0]
    sec, term = lax.axis_index("sec"), lax.axis_index("term")
    group = sectors * terms

    def peer(step):
        there = lax.rem(sec * terms + term + step, group)
        return {"sec": there // terms, "term": lax.rem(there, terms)}

    l_in = pltpu.make_async_copy(l_hbm.at[:, 0], l_buf.at[0], in_sem.at[0])
    r_in = pltpu.make_async_copy(r_hbm.at[:, 0], r_own, in_sem.at[1])
    x_in = pltpu.make_async_copy(
        x_hbm.at[:, 0, pl.ds(term * share, share)], x_buf, in_sem.at[2]
    )
    mask_in = pltpu.make_async_copy(mask_hbm, mask_ref, in_sem.at[3])
    mask_in.start()
    l_in.start()
    r_in.start()
    x_in.start()

    barrier = pltpu.get_barrier_semaphore()

    def greet(step):
        pl.semaphore_signal(barrier, inc=1, device_id=peer(step), device_id_type=MESH)

    each(group, greet, 1)

    mask_in.wait()
    l_in.wait()
    for k in range(ops):
        keep = mask_ref[0, k].astype(F32)
        l_buf[0, k] = (l_buf[0, k].astype(F32) * keep).astype(BF16)
    r_in.wait()
    pl.semaphore_wait(barrier, group - 1)

    owner = sec // share
    r_slot = lax.rem(owner - term + terms, terms) * share + lax.rem(sec, share)

    def r_copy(step, slot):
        return pltpu.make_async_remote_copy(
            src_ref=r_own,
            dst_ref=r_buf.at[slot],
            send_sem=r_send.at[step],
            recv_sem=r_recv.at[slot],
            device_id={"sec": lax.rem(sec + step, sectors), "term": owner},
            device_id_type=MESH,
        )

    def l_copy(step):
        return pltpu.make_async_remote_copy(
            src_ref=l_buf.at[0],
            dst_ref=l_buf.at[step],
            send_sem=l_send.at[step],
            recv_sem=l_recv.at[step],
            device_id={"sec": sec, "term": lax.rem(term + step, terms)},
            device_id_type=MESH,
        )

    each(sectors, lambda step: r_copy(step, r_slot).start(), 1)
    each(terms, lambda step: l_copy(step).start(), 1)

    @pl.when(owner != term)
    def _():
        r_copy(0, r_slot).start()

    @pl.when(owner == term)
    def _():
        pltpu.make_async_copy(r_own, r_buf.at[r_slot], r_recv.at[r_slot]).start()

    x_in.wait()
    x_wide = jnp.concatenate(
        [x_buf[v, b] for b in range(share) for v in range(vectors)], axis=1
    )

    def left(step):
        part = jnp.dot(
            l_buf[step].reshape(ops * size, size), x_wide, preferred_element_type=F32
        ).astype(BF16)
        for b in range(share):
            for v in range(vectors):
                at = (b * vectors + v) * size
                for k in range(ops):
                    t_buf[step, b, v * size:(v + 1) * size, k * size:(k + 1) * size] = part[
                        k * size:(k + 1) * size, at:at + size
                    ]

    left(0)
    for step in range(1, terms):
        l_copy(step).wait_recv()
        left(step)

    stat_rows = [jnp.zeros((1, size), F32)] * 8
    sigmas = []
    for b in range(share):
        sigma = jnp.zeros((vectors * size, size), F32)
        for step in range(terms):
            slot = step * share + b
            r_copy(0, slot).wait_recv()
            right = jnp.concatenate([r_buf[slot, k] for k in range(ops)], axis=1)
            sigma += lax.dot_general(
                t_buf[step, b], right, (((1,), (1,)), ((), ())), preferred_element_type=F32
            )
        sigmas.append(sigma)
        xs = [x_buf[v, b].astype(F32) for v in range(vectors)]
        for v in range(vectors):
            for w in range(vectors):
                stat_rows[v * vectors + w] += jnp.sum(
                    xs[v] * sigma[w * size:(w + 1) * size], axis=0, keepdims=True
                )
            stat_rows[vectors * vectors + v] += jnp.sum(xs[v] * xs[v], axis=0, keepdims=True)
    me = sec * terms + term
    sums = jnp.sum(jnp.concatenate(stat_rows, axis=0), axis=1, keepdims=True)
    here = lax.broadcasted_iota(jnp.int32, (8, size), 0)
    lane = lax.broadcasted_iota(jnp.int32, (8, size), 1)
    stat_buf[me] = jnp.sum(jnp.where(here == lane, sums, 0.0), axis=0, keepdims=True)

    def s_copy(step):
        return pltpu.make_async_remote_copy(
            src_ref=stat_buf.at[me],
            dst_ref=stat_buf.at[me],
            send_sem=s_send,
            recv_sem=s_recv,
            device_id=peer(step),
            device_id_type=MESH,
        )

    each(group, lambda step: s_copy(step).start(), 1)
    others = stat_buf.at[pl.ds(0, group - 1)]
    pltpu.make_async_copy(others, others, s_recv).wait()
    total = jnp.sum(stat_buf[...], axis=0) / F32(sectors * sectors * size * size)
    for v in range(vectors):
        sub_ref[v:v + 1, :] = total[:, v * vectors:(v + 1) * vectors]
    sub_out = pltpu.make_async_copy(sub_ref, sub_hbm, in_sem.at[1])
    sub_out.start()
    for v in range(vectors):
        own = v * vectors + v
        norm = vectors * vectors + v
        ritz = total[:, own:own + 1] / total[:, norm:norm + 1]
        for b in range(share):
            out_ref[v, b] = (
                sigmas[b][v * size:(v + 1) * size] - ritz * x_buf[v, b].astype(F32)
            ).astype(BF16)

    out = pltpu.make_async_copy(out_ref, out_hbm.at[:, 0], in_sem.at[0])
    out.start()

    each(sectors, lambda step: r_copy(step, r_slot).wait_send(), 1)
    each(terms, lambda step: l_copy(step).wait_send(), 1)
    pltpu.make_async_copy(others, others, s_send).wait()

    @pl.when(owner != term)
    def _():
        r_copy(0, r_slot).wait_send()

    sub_out.wait()
    out.wait()


def hand_on(res_in, sub_in, res_out, sub_out, res, sub, sem):
    res_load = pltpu.make_async_copy(res_in, res, sem.at[0])
    sub_load = pltpu.make_async_copy(sub_in, sub, sem.at[1])
    res_store = pltpu.make_async_copy(res, res_out, sem.at[2])
    sub_store = pltpu.make_async_copy(sub, sub_out, sem.at[3])
    res_load.start()
    sub_load.start()
    res_load.wait()
    res_store.start()
    sub_load.wait()
    sub_store.start()
    res_store.wait()
    sub_store.wait()


def local(sectors, terms, trial_vectors, left_ops, right_ops, term_mask):
    vectors, _, columns, size, _ = trial_vectors.shape
    ops = left_ops.shape[0]
    share = columns // terms
    group = sectors * terms
    hbm = pl.BlockSpec(memory_space=pltpu.HBM)
    made = (
        jax.ShapeDtypeStruct((vectors, 1, share, size, size), BF16),
        jax.ShapeDtypeStruct((vectors, vectors), F32),
    )
    results = pl.pallas_call(
        functools.partial(kernel, sectors, terms),
        out_shape=made,
        in_specs=[hbm] * 4,
        out_specs=(hbm, hbm),
        scratch_shapes=[
            pltpu.VMEM((vectors, share, size, size), BF16),
            pltpu.VMEM((vectors, vectors), F32),
            pltpu.SMEM((1, ops), jnp.int32),
            pltpu.VMEM((vectors, share, size, size), BF16),
            pltpu.VMEM((terms, ops, size, size), BF16),
            pltpu.VMEM((ops, size, size), BF16),
            pltpu.VMEM((terms * share, ops, size, size), BF16),
            pltpu.VMEM((terms, share, vectors * size, ops * size), BF16),
            pltpu.VMEM((group, 1, size), F32),
            pltpu.SemaphoreType.DMA((4,)),
            pltpu.SemaphoreType.DMA((terms,)),
            pltpu.SemaphoreType.DMA((terms,)),
            pltpu.SemaphoreType.DMA((sectors,)),
            pltpu.SemaphoreType.DMA((terms * share,)),
            pltpu.SemaphoreType.DMA,
            pltpu.SemaphoreType.DMA,
        ],
        compiler_params=pltpu.CompilerParams(
            collective_id=0, has_side_effects=True, vmem_limit_bytes=64 * 1024 * 1024
        ),
    )(trial_vectors, left_ops, right_ops, term_mask.T)
    return pl.pallas_call(
        hand_on,
        out_shape=made,
        in_specs=[hbm, hbm],
        out_specs=(hbm, hbm),
        scratch_shapes=[
            pltpu.VMEM(made[0].shape, BF16),
            pltpu.VMEM(made[1].shape, F32),
            pltpu.SemaphoreType.DMA((4,)),
        ],
        compiler_params=pltpu.CompilerParams(vmem_limit_bytes=64 * 1024 * 1024),
    )(*results)


def solution(mesh):
    placed = (
        P(None, ("grp", "sec"), None, None, None),
        P("term", ("grp", "sec"), None, None),
        P("term", ("grp", "sec"), None, None),
        P("term", ("grp", "sec")),
    )
    return jax.shard_map(
        functools.partial(local, mesh.shape["sec"], mesh.shape["term"]),
        mesh=mesh,
        in_specs=placed,
        out_specs=(P(None, ("grp", "sec"), "term", None, None), P("grp", None)),
        check_vma=False,
    )
```

```python
import functools

import jax
import jax.numpy as jnp
from jax import lax
from jax.experimental import pallas as pl
from jax.experimental.pallas import tpu as pltpu
from jax.sharding import PartitionSpec as P

MESH = pl.DeviceIdType.MESH
F32 = jnp.float32
BF16 = jnp.bfloat16


def each(count, body, first=0):
    if count - first <= 16:
        for index in range(first, count):
            body(index)
    else:
        lax.fori_loop(first, count, lambda index, carry: (body(index), carry)[1], 0)


def kernel(
    sectors, terms, x_hbm, l_hbm, r_hbm, mask_hbm, out_hbm, sub_hbm,
    out_ref, sub_ref, mask_ref, x_buf, l_buf, r_own, r_buf, t_buf, stat_buf,
    in_sem, l_send, l_recv, r_send, r_recv, s_send, s_recv,
):
    vectors, share, size = x_buf.shape[0], x_buf.shape[1], x_buf.shape[2]
    ops = r_own.shape[0]
    sec, term = lax.axis_index("sec"), lax.axis_index("term")
    group = sectors * terms

    def peer(step):
        there = lax.rem(sec * terms + term + step, group)
        return {"sec": there // terms, "term": lax.rem(there, terms)}

    l_in = pltpu.make_async_copy(l_hbm.at[:, 0], l_buf.at[0], in_sem.at[0])
    r_in = pltpu.make_async_copy(r_hbm.at[:, 0], r_own, in_sem.at[1])
    x_in = pltpu.make_async_copy(
        x_hbm.at[:, 0, pl.ds(term * share, share)], x_buf, in_sem.at[2]
    )
    mask_in = pltpu.make_async_copy(mask_hbm, mask_ref, in_sem.at[3])
    mask_in.start()
    l_in.start()
    r_in.start()
    x_in.start()

    barrier = pltpu.get_barrier_semaphore()

    def greet(step):
        pl.semaphore_signal(barrier, inc=1, device_id=peer(step), device_id_type=MESH)

    each(group, greet, 1)

    mask_in.wait()
    l_in.wait()
    for k in range(ops):
        keep = mask_ref[0, k].astype(F32)
        l_buf[0, k] = (l_buf[0, k].astype(F32) * keep).astype(BF16)
    r_in.wait()
    pl.semaphore_wait(barrier, group - 1)

    owner = sec // share
    r_slot = lax.rem(owner - term + terms, terms) * share + lax.rem(sec, share)

    def r_copy(step, slot):
        return pltpu.make_async_remote_copy(
            src_ref=r_own,
            dst_ref=r_buf.at[slot],
            send_sem=r_send.at[step],
            recv_sem=r_recv.at[slot],
            device_id={"sec": lax.rem(sec + step, sectors), "term": owner},
            device_id_type=MESH,
        )

    def l_copy(step):
        return pltpu.make_async_remote_copy(
            src_ref=l_buf.at[0],
            dst_ref=l_buf.at[step],
            send_sem=l_send.at[step],
            recv_sem=l_recv.at[step],
            device_id={"sec": sec, "term": lax.rem(term + step, terms)},
            device_id_type=MESH,
        )

    def r_start(step):
        turned = 1 + lax.rem(step - lax.rem(sec, 2), sectors - 1)
        r_copy(turned, r_slot).start()

    each(sectors, r_start, 1)
    each(terms, lambda step: l_copy(step).start(), 1)

    @pl.when(owner != term)
    def _():
        r_copy(0, r_slot).start()

    @pl.when(owner == term)
    def _():
        pltpu.make_async_copy(r_own, r_buf.at[r_slot], r_recv.at[r_slot]).start()

    x_in.wait()
    x_wide = jnp.concatenate(
        [x_buf[v, b] for b in range(share) for v in range(vectors)], axis=1
    )

    def left(step):
        part = jnp.dot(
            l_buf[step].reshape(ops * size, size), x_wide, preferred_element_type=F32
        ).astype(BF16)
        for b in range(share):
            for v in range(vectors):
                at = (b * vectors + v) * size
                for k in range(ops):
                    t_buf[step, b, v * size:(v + 1) * size, k * size:(k + 1) * size] = part[
                        k * size:(k + 1) * size, at:at + size
                    ]

    left(0)
    for step in range(1, terms):
        l_copy(step).wait_recv()
        left(step)

    stat_rows = [jnp.zeros((1, size), F32)] * 8
    sigmas = []
    for b in range(share):
        sigma = jnp.zeros((vectors * size, size), F32)
        for step in range(terms):
            slot = step * share + b
            r_copy(0, slot).wait_recv()
            right = jnp.concatenate([r_buf[slot, k] for k in range(ops)], axis=1)
            sigma += lax.dot_general(
                t_buf[step, b], right, (((1,), (1,)), ((), ())), preferred_element_type=F32
            )
        sigmas.append(sigma)
        xs = [x_buf[v, b].astype(F32) for v in range(vectors)]
        for v in range(vectors):
            for w in range(vectors):
                stat_rows[v * vectors + w] += jnp.sum(
                    xs[v] * sigma[w * size:(w + 1) * size], axis=0, keepdims=True
                )
            stat_rows[vectors * vectors + v] += jnp.sum(xs[v] * xs[v], axis=0, keepdims=True)
    me = sec * terms + term
    sums = jnp.sum(jnp.concatenate(stat_rows, axis=0), axis=1, keepdims=True)
    here = lax.broadcasted_iota(jnp.int32, (8, size), 0)
    lane = lax.broadcasted_iota(jnp.int32, (8, size), 1)
    stat_buf[me] = jnp.sum(jnp.where(here == lane, sums, 0.0), axis=0, keepdims=True)

    def s_copy(step):
        return pltpu.make_async_remote_copy(
            src_ref=stat_buf.at[me],
            dst_ref=stat_buf.at[me],
            send_sem=s_send,
            recv_sem=s_recv,
            device_id=peer(step),
            device_id_type=MESH,
        )

    each(group, lambda step: s_copy(step).start(), 1)
    others = stat_buf.at[pl.ds(0, group - 1)]
    pltpu.make_async_copy(others, others, s_recv).wait()
    total = jnp.sum(stat_buf[...], axis=0) / F32(sectors * sectors * size * size)
    for v in range(vectors):
        sub_ref[v:v + 1, :] = total[:, v * vectors:(v + 1) * vectors]
    sub_out = pltpu.make_async_copy(sub_ref, sub_hbm, in_sem.at[1])
    sub_out.start()
    for v in range(vectors):
        own = v * vectors + v
        norm = vectors * vectors + v
        ritz = total[:, own:own + 1] / total[:, norm:norm + 1]
        for b in range(share):
            out_ref[v, b] = (
                sigmas[b][v * size:(v + 1) * size] - ritz * x_buf[v, b].astype(F32)
            ).astype(BF16)

    out = pltpu.make_async_copy(out_ref, out_hbm.at[:, 0], in_sem.at[0])
    out.start()

    each(sectors, lambda step: r_copy(step, r_slot).wait_send(), 1)
    each(terms, lambda step: l_copy(step).wait_send(), 1)
    pltpu.make_async_copy(others, others, s_send).wait()

    @pl.when(owner != term)
    def _():
        r_copy(0, r_slot).wait_send()

    sub_out.wait()
    out.wait()


def hand_on(res_in, sub_in, res_out, sub_out, res, sub, sem):
    res_load = pltpu.make_async_copy(res_in, res, sem.at[0])
    sub_load = pltpu.make_async_copy(sub_in, sub, sem.at[1])
    res_store = pltpu.make_async_copy(res, res_out, sem.at[2])
    sub_store = pltpu.make_async_copy(sub, sub_out, sem.at[3])
    res_load.start()
    sub_load.start()
    res_load.wait()
    res_store.start()
    sub_load.wait()
    sub_store.start()
    res_store.wait()
    sub_store.wait()


def local(sectors, terms, trial_vectors, left_ops, right_ops, term_mask):
    vectors, _, columns, size, _ = trial_vectors.shape
    ops = left_ops.shape[0]
    share = columns // terms
    group = sectors * terms
    hbm = pl.BlockSpec(memory_space=pltpu.HBM)
    made = (
        jax.ShapeDtypeStruct((vectors, 1, share, size, size), BF16),
        jax.ShapeDtypeStruct((vectors, vectors), F32),
    )
    results = pl.pallas_call(
        functools.partial(kernel, sectors, terms),
        out_shape=made,
        in_specs=[hbm] * 4,
        out_specs=(hbm, hbm),
        scratch_shapes=[
            pltpu.VMEM((vectors, share, size, size), BF16),
            pltpu.VMEM((vectors, vectors), F32),
            pltpu.SMEM((1, ops), jnp.int32),
            pltpu.VMEM((vectors, share, size, size), BF16),
            pltpu.VMEM((terms, ops, size, size), BF16),
            pltpu.VMEM((ops, size, size), BF16),
            pltpu.VMEM((terms * share, ops, size, size), BF16),
            pltpu.VMEM((terms, share, vectors * size, ops * size), BF16),
            pltpu.VMEM((group, 1, size), F32),
            pltpu.SemaphoreType.DMA((4,)),
            pltpu.SemaphoreType.DMA((terms,)),
            pltpu.SemaphoreType.DMA((terms,)),
            pltpu.SemaphoreType.DMA((sectors,)),
            pltpu.SemaphoreType.DMA((terms * share,)),
            pltpu.SemaphoreType.DMA,
            pltpu.SemaphoreType.DMA,
        ],
        compiler_params=pltpu.CompilerParams(
            collective_id=0, has_side_effects=True, vmem_limit_bytes=64 * 1024 * 1024
        ),
    )(trial_vectors, left_ops, right_ops, term_mask.T)
    return pl.pallas_call(
        hand_on,
        out_shape=made,
        in_specs=[hbm, hbm],
        out_specs=(hbm, hbm),
        scratch_shapes=[
            pltpu.VMEM(made[0].shape, BF16),
            pltpu.VMEM(made[1].shape, F32),
            pltpu.SemaphoreType.DMA((4,)),
        ],
        compiler_params=pltpu.CompilerParams(vmem_limit_bytes=64 * 1024 * 1024),
    )(*results)


def solution(mesh):
    placed = (
        P(None, ("grp", "sec"), None, None, None),
        P("term", ("grp", "sec"), None, None),
        P("term", ("grp", "sec"), None, None),
        P("term", ("grp", "sec")),
    )
    return jax.shard_map(
        functools.partial(local, mesh.shape["sec"], mesh.shape["term"]),
        mesh=mesh,
        in_specs=placed,
        out_specs=(P(None, ("grp", "sec"), "term", None, None), P("grp", None)),
        check_vma=False,
    )
```
